256 devices in a mesh: tm: 32 (over z_hi, x, core), head: 8 (over z_lo, y).
Axes of the slice: x: 4, y: 4, z: 8 (z_hi: 4, z_lo: 2; z = z_hi * 2 + z_lo), core: 2. Of those that a mesh axis runs over, the one named last changes fastest.
Arguments:
- query_rows: bfloat16 [3, 16384, 4096], P(None, ('tm', 'head')), may hold values from -6 to 6
- key_rows: bfloat16 [3, 16384, 4096], P(None, ('tm', 'head')), may hold values from -6 to 6
- value_rows: bfloat16 [3, 16384, 4096], P(None, ('tm', 'head')), may hold values from -6 to 6
- step_rates: bfloat16 [3, 16384, 24], P(None, ('tm', 'head')), may hold values from 0.00048828125 to 0.005859375
- start_weights: float32 [32, 8, 3, 512, 512], P('tm', 'head'), may hold values from -0.25 to 0.25
Outputs:
- outputs: bfloat16 [3, 16384, 4096], P(None, ('tm', 'head'))
- final_weights: float32 [32, 8, 3, 512, 512], P('tm', 'head')
The draws below stay inside these ranges and needn't reach their ends.
All inputs are finite; a program needn't handle non-finite values.
Results may differ from the reference program's by a relative error of at most 0.04.
Values may be sent and summed in bfloat16 or wider, within the bound.
No kernel may reach another device: no remote copies, remote signals or barrier semaphores. Data moves between devices by JAX's collectives and lax.ppermute only.
A program may use at most 128 MiB of HBM per device.

```python
import math
import jax
import jax.numpy as jnp
from jax import lax

D = 512
H = 8
GROUP = 512
TICKS = 3
TOKENS = 16384
N_TM = 32


def steps_of(own_key, extent, cuts, low, top_value):
    gain, own = 1.0, jax.random.fold_in(own_key, 6)
    for position, blocks in cuts:
        steps = jnp.exp(jax.random.uniform(jax.random.fold_in(own, position), (blocks,), jnp.float32, low / len(cuts), top_value / len(cuts)))
        gain = gain * jnp.repeat(steps, extent[position] // blocks).reshape([-1 if axis == position else 1 for axis in range(len(extent))])
    return gain


def bell_draw(rng, extent, spread, most, cuts=(), kind=jnp.bfloat16):
    level = steps_of(rng, extent, cuts, -0.22, 0.18) if cuts else 1.0
    values = jax.random.normal(rng, extent, jnp.float32) * spread * level
    return jnp.minimum(jnp.maximum(values, -most), most).astype(kind)


def setup_inputs(seed: int = 0) -> dict:
    seeds = jax.random.split(jax.random.key(seed), 6)
    return {
        "query_rows": bell_draw(seeds[0], (TICKS, TOKENS, H * D), 1.0, 6.0, ((1, 256),)),
        "key_rows": bell_draw(seeds[1], (TICKS, TOKENS, H * D), 1.0, 6.0, ((1, 256),)),
        "value_rows": bell_draw(seeds[2], (TICKS, TOKENS, H * D), 1.0, 6.0, ((1, 256),)),
        "step_rates": jnp.clip(jnp.exp(math.log(0.005859375) - 2.4849066 * jax.random.uniform(seeds[3], (TICKS, TOKENS, 3 * H), jnp.float32) ** steps_of(seeds[3], (TICKS, TOKENS, 3 * H), ((1, 256),), -0.2, 0.2)), 0.00048828125, 0.005859375).astype(jnp.bfloat16),
        "start_weights": bell_draw(seeds[4], (N_TM, H, 3, D, D), D ** -0.5, 0.25, ((0, 32), (1, 8)), jnp.float32),
    }


def product(left, right):
    return jnp.dot(left.astype(jnp.float32), right.astype(jnp.float32), preferred_element_type=jnp.float32)


def swish_parts(inputs):
    sigmoid_value = jax.nn.sigmoid(inputs)
    return inputs * sigmoid_value, sigmoid_value


def apply_head(rounded, query_block):
    gate_part = product(query_block, rounded[0])
    up_part = product(query_block, rounded[1])
    hidden = (swish_parts(gate_part)[0] * up_part).astype(jnp.bfloat16)
    return product(hidden, rounded[2]).astype(jnp.bfloat16)


def update_head(weights, rounded, key_block, value_block, rate_block):
    pre_gate = product(key_block, rounded[0])
    pre_up = product(key_block, rounded[1])
    activated, sigmoid_value = swish_parts(pre_gate)
    hidden = (activated * pre_up).astype(jnp.bfloat16)
    upstream = product(value_block, rounded[2].T)
    rate_values = rate_block.astype(jnp.float32)
    gate_error = (rate_values[:, 0:1] * upstream * pre_up * sigmoid_value * (1.0 + pre_gate * (1.0 - sigmoid_value))).astype(jnp.bfloat16)
    up_error = (rate_values[:, 1:2] * upstream * activated).astype(jnp.bfloat16)
    out_error = (rate_values[:, 2:3] * value_block.astype(jnp.float32)).astype(jnp.bfloat16)
    increment = jnp.stack([product(key_block.T, gate_error), product(key_block.T, up_error), product(hidden.T, out_error)])
    return weights + increment


def block_tick(inputs):
    weights, query_block, key_block, value_block, rate_block = inputs
    rounded = weights.astype(jnp.bfloat16)
    return apply_head(rounded, query_block), update_head(weights, rounded, key_block, value_block, rate_block)


def reference(query_rows, key_rows, value_rows, step_rates, start_weights):
    heads_tick = jax.vmap(block_tick)
    carried = start_weights
    results = []
    updated = start_weights
    for tick_index in range(TICKS):
        def arrange(source, columns):
            return source[tick_index].reshape(N_TM, GROUP, H, columns).transpose(0, 2, 1, 3)

        emitted, updated = lax.map(heads_tick, (carried, arrange(query_rows, D), arrange(key_rows, D), arrange(value_rows, D), arrange(step_rates, 3)))
        results.append(emitted.transpose(0, 2, 1, 3).reshape(N_TM * GROUP, H * D))
        carried = jnp.concatenate([start_weights[:1], updated[:-1]], axis=0)
    return jnp.stack(results), updated
```

```python
import functools

import jax
import jax.numpy as jnp
from jax import lax
from jax.experimental import pallas as pl
from jax.experimental.pallas import tpu as pltpu
from jax.sharding import PartitionSpec as P

HEADS = 8
ROWS = 64
WIDTH = 512
TOKENS = HEADS * ROWS
RATE_ROWS = 16
HALF = TOKENS // 2
F32 = jnp.float32
BF16 = jnp.bfloat16
MIB = 1024 * 1024
HBM = pl.BlockSpec(memory_space=pltpu.HBM)


def run_copies(pairs, sems):
    copies = [pltpu.make_async_copy(src, dst, sems.at[i]) for i, (src, dst) in enumerate(pairs)]
    for copy in copies:
        copy.start()
    return copies


def wait_all(copies):
    for copy in copies:
        copy.wait()


def head_columns(head):
    return pl.ds(head * WIDTH, WIDTH)


def slot(index):
    return pl.ds(index * ROWS, ROWS)


def pack_first(keys, values, rates, sent, staged, rate_rows, rate_sent, load, store):
    loads = run_copies([(keys.at[0], staged.at[0]), (values.at[0], staged.at[1])], load)
    rate_rows[...] = jnp.zeros_like(rate_rows)
    for tick in range(3):
        turned = rates[tick].astype(F32).T
        for head in range(HEADS):
            rate_rows[head, 3 * tick : 3 * tick + 3, 0:ROWS] = turned[3 * head : 3 * head + 3, :]
    rate_sent[...] = rate_rows[...].astype(BF16)
    stores = run_copies([(rate_sent, sent.at[:, pl.ds(2 * ROWS, RATE_ROWS), :])], store)
    for place in range(2):
        loads[place].wait()
        for head in range(HEADS):
            copy = pltpu.make_async_copy(
                staged.at[place, :, head_columns(head)],
                sent.at[head, slot(place), :],
                store.at[1 + place * HEADS + head],
            )
            copy.start()
            stores.append(copy)
    wait_all(stores)


def send_first(keys, values, rates):
    return pl.pallas_call(
        pack_first,
        out_shape=pltpu.HBM((HEADS, 2 * ROWS + RATE_ROWS, WIDTH), BF16),
        in_specs=[HBM, HBM, pl.BlockSpec(memory_space=pltpu.VMEM)],
        out_specs=HBM,
        scratch_shapes=[
            pltpu.VMEM((2, ROWS, HEADS * WIDTH), BF16),
            pltpu.VMEM((HEADS, RATE_ROWS, WIDTH), F32),
            pltpu.VMEM((HEADS, RATE_ROWS, WIDTH), BF16),
            pltpu.SemaphoreType.DMA((2,)),
            pltpu.SemaphoreType.DMA((2 * HEADS + 1,)),
        ],
        cost_estimate=pl.CostEstimate(flops=0, bytes_accessed=2 * MIB, transcendentals=0),
        name="pack_first",
    )(keys, values, rates)


def pack_rest(queries, keys, values, second, third, staged, load, store):
    plan = (
        (second, 0, keys, 1),
        (second, 1, values, 1),
        (third, 0, keys, 2),
        (third, 1, values, 2),
        (third, 2, queries, 0),
        (third, 3, queries, 1),
        (third, 4, queries, 2),
    )
    loads = run_copies([(source.at[tick], staged.at[i]) for i, (_, _, source, tick) in enumerate(plan)], load)
    stores = []
    for i, (target, place, _, _) in enumerate(plan):
        loads[i].wait()
        for head in range(HEADS):
            copy = pltpu.make_async_copy(
                staged.at[i, :, head_columns(head)], target.at[head, slot(place), :], store.at[i * HEADS + head]
            )
            copy.start()
            stores.append(copy)
    wait_all(stores)


def send_rest(queries, keys, values):
    return pl.pallas_call(
        pack_rest,
        out_shape=(
            pltpu.HBM((HEADS, 2 * ROWS, WIDTH), BF16),
            pltpu.HBM((HEADS, 5 * ROWS, WIDTH), BF16),
        ),
        in_specs=[HBM] * 3,
        out_specs=(HBM, HBM),
        scratch_shapes=[
            pltpu.VMEM((7, ROWS, HEADS * WIDTH), BF16),
            pltpu.SemaphoreType.DMA((7,)),
            pltpu.SemaphoreType.DMA((7 * HEADS,)),
        ],
        cost_estimate=pl.CostEstimate(flops=0, bytes_accessed=7 * MIB, transcendentals=0),
        name="pack_rest",
    )(queries, keys, values)


def unpack_outputs(received, result, staged, load, store):
    loads = run_copies(
        [
            (received.at[head, slot(tick), :], staged.at[tick, :, head_columns(head)])
            for tick in range(3)
            for head in range(HEADS)
        ],
        load,
    )
    stores = []
    for tick in range(3):
        wait_all(loads[tick * HEADS : (tick + 1) * HEADS])
        copy = pltpu.make_async_copy(staged.at[tick], result.at[tick], store.at[tick])
        copy.start()
        stores.append(copy)
    wait_all(stores)


def place_outputs(received):
    return pl.pallas_call(
        unpack_outputs,
        out_shape=pltpu.HBM((3, ROWS, HEADS * WIDTH), BF16),
        in_specs=[HBM],
        out_specs=HBM,
        scratch_shapes=[
            pltpu.VMEM((3, ROWS, HEADS * WIDTH), BF16),
            pltpu.SemaphoreType.DMA((3 * HEADS,)),
            pltpu.SemaphoreType.DMA((3,)),
        ],
        cost_estimate=pl.CostEstimate(flops=0, bytes_accessed=3 * MIB, transcendentals=0),
        name="unpack_outputs",
    )(received)


def dot(left, right, left_dim=1, right_dim=0):
    return lax.dot_general(left, right, (((left_dim,), (right_dim,)), ((), ())), preferred_element_type=F32)


def rate_columns(rates, tick, first_source, sources):
    parts = []
    for source in range(first_source, first_source + sources):
        turned = rates[source, :, 0:128].astype(F32).T
        parts.append(turned[0:ROWS, 3 * tick : 3 * tick + 3])
    return jnp.concatenate(parts, axis=0)


def errors_of(rounded, pair, rates, tick, work):
    gate_error, up_error, hidden, out_error = work
    for half in range(2):
        sources = pl.ds(half * 4, 4)
        rows = pl.ds(half * HALF, HALF)
        keys = pair[sources, 0:ROWS, :].reshape(HALF, WIDTH)
        values = pair[sources, ROWS : 2 * ROWS, :].reshape(HALF, WIDTH)
        rate = rate_columns(rates, tick, half * 4, 4)
        pre_gate = dot(keys, rounded[0])
        pre_up = dot(keys, rounded[1])
        upstream = dot(values, rounded[2], 1, 1)
        sigmoid_value = jax.nn.sigmoid(pre_gate)
        activated = pre_gate * sigmoid_value
        hidden[rows, :] = (activated * pre_up).astype(BF16)
        gate_error[rows, :] = (
            rate[:, 0:1] * upstream * pre_up * sigmoid_value * (1.0 + pre_gate * (1.0 - sigmoid_value))
        ).astype(BF16)
        up_error[rows, :] = (rate[:, 1:2] * upstream * activated).astype(BF16)
        out_error[rows, :] = (rate[:, 2:3] * values.astype(F32)).astype(BF16)


def write_updates(added, pair, work, fresh, out, sems):
    gate_error, up_error, hidden, out_error = work
    copies = []
    for half in range(2):
        columns = pl.ds(half * HALF, HALF)
        keys = pair[:, 0:ROWS, columns].reshape(TOKENS, HALF)
        steps = (
            (keys, gate_error),
            (keys, up_error),
            (hidden[:, columns], out_error),
        )
        for index, (left, right) in enumerate(steps):
            value = added[index, columns, :].astype(F32) + dot(left, right[...], 0, 0)
            fresh[index, columns, :] = value.astype(fresh.dtype)
            copy = pltpu.make_async_copy(
                fresh.at[index, columns, :], out.at[index, columns, :], sems.at[half * 3 + index]
            )
            copy.start()
            copies.append(copy)
    wait_all(copies)


WORK = [pltpu.VMEM((TOKENS, WIDTH), BF16)] * 4


def start_update(start, received, out, pair, wide, rounded, fresh, e0, e1, hid, e2, sems, load):
    copies = run_copies([(received, pair), (start, wide)], load)
    wait_all(copies)
    rounded[...] = wide[...].astype(BF16)
    work = (e0, e1, hid, e2)
    errors_of(rounded, pair.at[:, 0 : 2 * ROWS, :], pair.at[:, 2 * ROWS :, :], 0, work)
    write_updates(wide, pair, work, fresh, out, sems)


def update_start(start, received):
    return pl.pallas_call(
        start_update,
        out_shape=pltpu.HBM((3, WIDTH, WIDTH), BF16),
        in_specs=[HBM, HBM],
        out_specs=HBM,
        scratch_shapes=[
            pltpu.VMEM((HEADS, 2 * ROWS + RATE_ROWS, WIDTH), BF16),
            pltpu.VMEM((3, WIDTH, WIDTH), F32),
            pltpu.VMEM((3, WIDTH, WIDTH), BF16),
            pltpu.VMEM((3, WIDTH, WIDTH), BF16),
            *WORK,
            pltpu.SemaphoreType.DMA((6,)),
            pltpu.SemaphoreType.DMA((2,)),
        ],
        compiler_params=pltpu.CompilerParams(vmem_limit_bytes=40 * MIB),
        cost_estimate=pl.CostEstimate(flops=0, bytes_accessed=0, transcendentals=0),
        name="update_start",
    )(start, received)


def fetch_weights(start, from_core, from_chip, rounded, load):
    place = lax.axis_index("tm")
    odd = lax.rem(place, 2) == 1
    if from_core is not None:

        @pl.when(odd)
        def _():
            copy = pltpu.make_async_copy(from_core, rounded, load)
            copy.start()
            copy.wait()

    if from_chip is not None:

        @pl.when(jnp.logical_and(jnp.logical_not(odd), place > 0))
        def _():
            copy = pltpu.make_async_copy(from_chip, rounded, load)
            copy.start()
            copy.wait()

        @pl.when(place == 0)
        def _():
            def with_start(wide):
                copy = pltpu.make_async_copy(start, wide, load)
                copy.start()
                copy.wait()
                rounded[...] = wide[...].astype(BF16)

            pl.run_scoped(with_start, pltpu.VMEM((3, WIDTH, WIDTH), F32))


def later_update(cores, tick, *refs):
    refs = list(refs)
    start = refs.pop(0)
    from_core = refs.pop(0) if cores in (1, None) else None
    from_chip = refs.pop(0) if cores in (0, None) else None
    received, first, out, pair, rates, rounded, fresh, e0, e1, hid, e2, sems, load = refs

    def run():
        copies = run_copies(
            [
                (received.at[:, pl.ds(0, 2 * ROWS), :], pair),
                (first.at[:, pl.ds(2 * ROWS, RATE_ROWS), :], rates),
            ],
            load,
        )
        fetch_weights(start, from_core, from_chip, rounded, load.at[2])
        wait_all(copies)
        work = (e0, e1, hid, e2)
        errors_of(rounded, pair, rates, tick, work)
        write_updates(rounded, pair, work, fresh, out, sems)

    if cores is None:
        run()
    else:
        pl.when(lax.rem(lax.axis_index("tm"), 2) == cores)(run)


def update_later(cores, tick, kind, start, weights, received, first):
    operands = [start, *weights, received, first]
    return pl.pallas_call(
        functools.partial(later_update, cores, tick),
        out_shape=pltpu.HBM((3, WIDTH, WIDTH), kind),
        in_specs=[HBM] * len(operands),
        out_specs=HBM,
        scratch_shapes=[
            pltpu.VMEM((HEADS, 2 * ROWS, WIDTH), BF16),
            pltpu.VMEM((HEADS, RATE_ROWS, WIDTH), BF16),
            pltpu.VMEM((3, WIDTH, WIDTH), BF16),
            pltpu.VMEM((3, WIDTH, WIDTH), kind),
            *WORK,
            pltpu.SemaphoreType.DMA((6,)),
            pltpu.SemaphoreType.DMA((3,)),
        ],
        compiler_params=pltpu.CompilerParams(vmem_limit_bytes=40 * MIB),
        cost_estimate=pl.CostEstimate(flops=0, bytes_accessed=0, transcendentals=0),
        name="update_tick%d_%s" % (tick, {0: "even", 1: "odd", None: "all"}[cores]),
    )(*operands)


def apply_weights(rounded, query, produced):
    for half in range(2):
        sources = pl.ds(half * 4, 4)
        queries = query[sources, :, :].reshape(HALF, WIDTH)
        gate_part = dot(queries, rounded[0])
        up_part = dot(queries, rounded[1])
        hidden = (gate_part * jax.nn.sigmoid(gate_part) * up_part).astype(BF16)
        produced[sources, :, :] = dot(hidden, rounded[2]).astype(BF16).reshape(4, ROWS, WIDTH)


def early_apply(start, from_core, from_chip, received, out, query, wide, rounded, produced, sems):
    copies = run_copies(
        [
            (received.at[:, slot(2), :], query.at[0]),
            (received.at[:, slot(3), :], query.at[1]),
            (start, wide),
        ],
        sems,
    )
    wait_all(copies)
    rounded[...] = wide[...].astype(BF16)
    apply_weights(rounded, query.at[0], produced.at[0])
    first = pltpu.make_async_copy(produced.at[0], out.at[:, slot(0), :], sems.at[0])
    first.start()
    fetch_weights(start, from_core, from_chip, rounded, sems.at[2])
    apply_weights(rounded, query.at[1], produced.at[1])
    second = pltpu.make_async_copy(produced.at[1], out.at[:, slot(1), :], sems.at[1])
    second.start()
    first.wait()
    second.wait()


def apply_early(start, from_core, from_chip, received):
    return pl.pallas_call(
        early_apply,
        out_shape=pltpu.HBM((HEADS, 3 * ROWS, WIDTH), BF16),
        in_specs=[HBM] * 4,
        out_specs=HBM,
        scratch_shapes=[
            pltpu.VMEM((2, HEADS, ROWS, WIDTH), BF16),
            pltpu.VMEM((3, WIDTH, WIDTH), F32),
            pltpu.VMEM((3, WIDTH, WIDTH), BF16),
            pltpu.VMEM((2, HEADS, ROWS, WIDTH), BF16),
            pltpu.SemaphoreType.DMA((3,)),
        ],
        compiler_params=pltpu.CompilerParams(vmem_limit_bytes=40 * MIB),
        cost_estimate=pl.CostEstimate(flops=0, bytes_accessed=0, transcendentals=0),
        name="apply_ticks01",
    )(start, from_core, from_chip, received)


def late_apply(start, from_core, from_chip, received, held, out, query, rounded, produced, sems):
    del held
    copy = pltpu.make_async_copy(received.at[:, slot(4), :], query, sems.at[0])
    copy.start()
    fetch_weights(start, from_core, from_chip, rounded, sems.at[1])
    copy.wait()
    apply_weights(rounded, query, produced)
    last = pltpu.make_async_copy(produced, out.at[:, slot(2), :], sems.at[0])
    last.start()
    last.wait()


def apply_late(start, from_core, from_chip, received, held):
    return pl.pallas_call(
        late_apply,
        out_shape=pltpu.HBM((HEADS, 3 * ROWS, WIDTH), BF16),
        in_specs=[HBM] * 5,
        out_specs=HBM,
        scratch_shapes=[
            pltpu.VMEM((HEADS, ROWS, WIDTH), BF16),
            pltpu.VMEM((3, WIDTH, WIDTH), BF16),
            pltpu.VMEM((HEADS, ROWS, WIDTH), BF16),
            pltpu.SemaphoreType.DMA((2,)),
        ],
        input_output_aliases={4: 0},
        compiler_params=pltpu.CompilerParams(vmem_limit_bytes=40 * MIB),
        cost_estimate=pl.CostEstimate(flops=0, bytes_accessed=0, transcendentals=0),
        name="apply_tick2",
    )(start, from_core, from_chip, received, held)


def exchange(block):
    return lax.all_to_all(block, "head", split_axis=0, concat_axis=0, tiled=True)


def after(*arrays):
    return lax.optimization_barrier(arrays)


def on_device(query_rows, key_rows, value_rows, step_rates, start_weights):
    start = start_weights[0, 0]
    places = lax.axis_size("tm")
    to_core = [(i, i + 1) for i in range(0, places, 2)]
    to_chip = [(i, i + 1) for i in range(1, places - 1, 2)]

    first_sent = send_first(key_rows, value_rows, step_rates)
    first = exchange(first_sent)
    query_rows, key_rows, value_rows, _ = after(query_rows, key_rows, value_rows, first_sent)
    second_sent, third_sent = send_rest(query_rows, key_rows, value_rows)
    fresh0 = update_start(start, first)
    core1 = lax.ppermute(fresh0, "tm", to_core)
    chip1 = lax.ppermute(fresh0, "tm", to_chip)
    second_sent, _ = after(second_sent, fresh0)
    second = exchange(second_sent)
    fresh1_odd = update_later(1, 1, BF16, start, [core1], second, first)
    third_sent, chip1, _ = after(third_sent, chip1, fresh1_odd)
    third = exchange(third_sent)
    fresh1_even = update_later(0, 1, BF16, start, [chip1], second, first)
    core2 = lax.ppermute(fresh1_even, "tm", to_core)
    chip2 = lax.ppermute(fresh1_odd, "tm", to_chip)
    third, _ = after(third, fresh1_even)
    held = apply_early(start, core1, chip1, third)
    held = apply_late(start, core2, chip2, third, held)
    returned = exchange(held)
    final = update_later(None, 2, F32, start, [core2, chip2], third, first)
    return place_outputs(returned), final[None, None]


def solution(mesh):
    return jax.shard_map(
        on_device,
        mesh=mesh,
        in_specs=(
            P(None, ("tm", "head"), None),
            P(None, ("tm", "head"), None),
            P(None, ("tm", "head"), None),
            P(None, ("tm", "head"), None),
            P("tm", "head", None, None, None),
        ),
        out_specs=(P(None, ("tm", "head"), None), P("tm", "head", None, None, None)),
        check_vma=False,
    )
```

```python
import functools

import jax
import jax.numpy as jnp
from jax import lax
from jax.experimental import pallas as pl
from jax.experimental.pallas import tpu as pltpu
from jax.sharding import PartitionSpec as P

HEADS = 8
ROWS = 64
WIDTH = 512
TOKENS = HEADS * ROWS
RATE_ROWS = 16
HALF = TOKENS // 2
F32 = jnp.float32
BF16 = jnp.bfloat16
MIB = 1024 * 1024
FREE = pl.CostEstimate(flops=0, bytes_accessed=0, transcendentals=0)
PLANE = 8
ANY = pl.BlockSpec(memory_space=pl.ANY)
HBM = pl.BlockSpec(memory_space=pltpu.HBM)


def run_copies(pairs, sems):
    copies = [pltpu.make_async_copy(src, dst, sems.at[i]) for i, (src, dst) in enumerate(pairs)]
    for copy in copies:
        copy.start()
    return copies


def wait_all(copies):
    for copy in copies:
        copy.wait()


def head_columns(head):
    return pl.ds(head * WIDTH, WIDTH)


def slot(index):
    return pl.ds(index * ROWS, ROWS)


def pack_arrays(plan, staged, load, store):
    loads = run_copies([(source.at[tick], staged.at[i]) for i, (source, tick, _, _) in enumerate(plan)], load)
    stores = []
    for i, (_, _, target, place) in enumerate(plan):
        loads[i].wait()
        for head in range(HEADS):
            copy = pltpu.make_async_copy(
                staged.at[i, :, head_columns(head)], target.at[head, slot(place), :], store.at[i * HEADS + head]
            )
            copy.start()
            stores.append(copy)
    return stores


def pack_first(keys, values, rates, sent, staged, rate_rows, rate_sent, load, store):
    plan = ((keys, 0, sent, 0), (values, 0, sent, 1), (keys, 1, sent, 2), (values, 1, sent, 3))
    stores = pack_arrays(plan, staged, load, store)
    rate_rows[...] = jnp.zeros_like(rate_rows)
    for tick in range(3):
        turned = rates[tick].astype(F32)
        for head in range(HEADS):
            rate_rows[head, 3 * tick : 3 * tick + 3, 0:ROWS] = turned[3 * head : 3 * head + 3, :]
    rate_sent[...] = rate_rows[...].astype(BF16)
    last = pltpu.make_async_copy(rate_sent, sent.at[:, pl.ds(4 * ROWS, RATE_ROWS), :], store.at[4 * HEADS])
    last.start()
    wait_all(stores)
    last.wait()


def send_first(keys, values, rates):
    return pl.pallas_call(
        pack_first,
        out_shape=pltpu.HBM((HEADS, 4 * ROWS + RATE_ROWS, WIDTH), BF16),
        in_specs=[HBM, HBM, pl.BlockSpec(memory_space=pltpu.VMEM)],
        out_specs=HBM,
        scratch_shapes=[
            pltpu.VMEM((4, ROWS, HEADS * WIDTH), BF16),
            pltpu.VMEM((HEADS, RATE_ROWS, WIDTH), F32),
            pltpu.VMEM((HEADS, RATE_ROWS, WIDTH), BF16),
            pltpu.SemaphoreType.DMA((4,)),
            pltpu.SemaphoreType.DMA((4 * HEADS + 1,)),
        ],
        cost_estimate=FREE,
        name="pack_first",
    )(keys, values, rates)


def pack_rest(queries, keys, values, sent, staged, load, store):
    plan = (
        (queries, 0, sent, 0),
        (queries, 1, sent, 1),
        (queries, 2, sent, 2),
        (keys, 2, sent, 3),
        (values, 2, sent, 4),
    )
    wait_all(pack_arrays(plan, staged, load, store))


def send_rest(queries, keys, values):
    return pl.pallas_call(
        pack_rest,
        out_shape=pltpu.HBM((HEADS, 5 * ROWS, WIDTH), BF16),
        in_specs=[HBM] * 3,
        out_specs=HBM,
        scratch_shapes=[
            pltpu.VMEM((5, ROWS, HEADS * WIDTH), BF16),
            pltpu.SemaphoreType.DMA((5,)),
            pltpu.SemaphoreType.DMA((5 * HEADS,)),
        ],
        cost_estimate=FREE,
        name="pack_rest",
    )(queries, keys, values)


def unpack_arrays(plan, staged, load, store):
    loads = run_copies(
        [
            (source.at[head, slot(place), :], staged.at[i, :, head_columns(head)])
            for i, (source, place, _, _) in enumerate(plan)
            for head in range(HEADS)
        ],
        load,
    )
    stores = []
    for i, (_, _, target, tick) in enumerate(plan):
        wait_all(loads[i * HEADS : (i + 1) * HEADS])
        copy = pltpu.make_async_copy(staged.at[i], target.at[tick], store.at[i])
        copy.start()
        stores.append(copy)
    wait_all(stores)


def unpack_outputs(received, result, staged, load, store):
    unpack_arrays([(received, tick, result, tick) for tick in range(3)], staged, load, store)


def place_outputs(received):
    return pl.pallas_call(
        unpack_outputs,
        out_shape=pltpu.HBM((3, ROWS, HEADS * WIDTH), BF16),
        in_specs=[ANY],
        out_specs=HBM,
        scratch_shapes=[
            pltpu.VMEM((3, ROWS, HEADS * WIDTH), BF16),
            pltpu.SemaphoreType.DMA((3 * HEADS,)),
            pltpu.SemaphoreType.DMA((3,)),
        ],
        cost_estimate=FREE,
        name="unpack_outputs",
    )(received)


def dot(left, right, left_dim=1, right_dim=0):
    return lax.dot_general(left, right, (((left_dim,), (right_dim,)), ((), ())), preferred_element_type=F32)


def rate_columns(rates, tick, first_source, sources):
    parts = []
    for source in range(first_source, first_source + sources):
        turned = rates[source, :, 0:128].astype(F32).T
        parts.append(turned[0:ROWS, 3 * tick : 3 * tick + 3])
    return jnp.concatenate(parts, axis=0)


def errors_of(rounded, pair, rates, tick, work):
    gate_error, up_error, hidden, out_error = work
    for half in range(2):
        sources = pl.ds(half * 4, 4)
        rows = pl.ds(half * HALF, HALF)
        keys = pair[sources, 0:ROWS, :].reshape(HALF, WIDTH)
        values = pair[sources, ROWS : 2 * ROWS, :].reshape(HALF, WIDTH)
        rate = rate_columns(rates, tick, half * 4, 4)
        pre_gate = dot(keys, rounded[0])
        pre_up = dot(keys, rounded[1])
        upstream = dot(values, rounded[2], 1, 1)
        sigmoid_value = jax.nn.sigmoid(pre_gate)
        activated = pre_gate * sigmoid_value
        hidden[rows, :] = (activated * pre_up).astype(BF16)
        gate_error[rows, :] = (
            rate[:, 0:1] * upstream * pre_up * sigmoid_value * (1.0 + pre_gate * (1.0 - sigmoid_value))
        ).astype(BF16)
        up_error[rows, :] = (rate[:, 1:2] * upstream * activated).astype(BF16)
        out_error[rows, :] = (rate[:, 2:3] * values.astype(F32)).astype(BF16)


def is_odd():
    return lax.rem(lax.axis_index("tm"), 2) == 1


STACK = (3, WIDTH, WIDTH)
PARTS = ((WIDTH, WIDTH), (2 * WIDTH, WIDTH))
TOKEN = pltpu.HBM((8, 128), F32)


def piece(parts, index, half):
    if index == 0:
        return parts[0].at[pl.ds(half * HALF, HALF), :]
    return parts[1].at[pl.ds((index - 1) * WIDTH + half * HALF, HALF), :]


def stack_piece(stack, index, half):
    return stack.at[index, pl.ds(half * HALF, HALF), :]


def write_updates(added, pair, work, fresh, routes, sems):
    gate_error, up_error, hidden, out_error = work
    started = []
    for index in (1, 2, 0):
        for half in range(2):
            columns = pl.ds(half * HALF, HALF)
            keys = pair[:, 0:ROWS, columns].reshape(TOKENS, HALF)
            left, right = ((keys, gate_error), (keys, up_error), (hidden[:, columns], out_error))[index]
            value = added[index, columns, :].astype(F32) + dot(left, right[...], 0, 0)
            fresh[index, columns, :] = value.astype(fresh.dtype)
            for predicate, target in routes:
                copy = pltpu.make_async_copy(
                    fresh.at[index, columns, :], target(index, half), sems.at[half * 3 + index]
                )
                if predicate is None:
                    copy.start()
                else:
                    pl.when(predicate)(copy.start)
                started.append((predicate, copy))
    for predicate, copy in started:
        if predicate is None:
            copy.wait()
        else:
            pl.when(predicate)(copy.wait)


WORK = [pltpu.VMEM((TOKENS, WIDTH), BF16)] * 4


def start_update(start, received, stacked, part0, part1, pair, rates, wide, rounded, fresh, e0, e1, hid, e2, sems, load):
    copies = run_copies(
        [
            (start, wide),
            (received.at[:, pl.ds(0, 2 * ROWS), :], pair),
            (received.at[:, pl.ds(4 * ROWS, RATE_ROWS), :], rates),
        ],
        load,
    )
    copies[0].wait()
    rounded[...] = wide[...].astype(BF16)
    wait_all(copies[1:])
    work = (e0, e1, hid, e2)
    errors_of(rounded, pair, rates, 0, work)
    odd = is_odd()
    routes = (
        (odd, functools.partial(piece, (part0, part1))),
        (jnp.logical_not(odd), functools.partial(stack_piece, stacked)),
    )
    write_updates(wide, pair, work, fresh, routes, sems)


def update_start(start, received):
    return pl.pallas_call(
        start_update,
        out_shape=tuple(pltpu.HBM(shape, BF16) for shape in (STACK, *PARTS)),
        in_specs=[ANY, ANY],
        out_specs=(HBM,) * 3,
        scratch_shapes=[
            pltpu.VMEM((HEADS, 2 * ROWS, WIDTH), BF16),
            pltpu.VMEM((HEADS, RATE_ROWS, WIDTH), BF16),
            pltpu.VMEM(STACK, F32),
            pltpu.VMEM(STACK, BF16),
            pltpu.VMEM(STACK, BF16),
            *WORK,
            pltpu.SemaphoreType.DMA((6,)),
            pltpu.SemaphoreType.DMA((3,)),
        ],
        compiler_params=pltpu.CompilerParams(vmem_limit_bytes=40 * MIB),
        cost_estimate=FREE,
        name="update_start",
    )(start, received)


def fetch_from_chip(start, from_chip, rounded, load):
    place = lax.axis_index("tm")
    crossed = lax.rem(place, PLANE) == 0
    direct, straight, relayed = from_chip

    def gather(parts):
        order = ((0, 0), (0, 1), (1, 0), (1, 1), (2, 0), (2, 1))
        wait_all(run_copies([(piece(parts, *which), stack_piece(rounded, *which)) for which in order], load))

    pl.when(jnp.logical_not(crossed))(lambda: gather((direct, straight)))
    pl.when(jnp.logical_and(crossed, place > 0))(lambda: gather((direct, relayed)))

    @pl.when(place == 0)
    def _():
        def with_start(wide):
            wait_all(run_copies([(start, wide)], load))
            rounded[...] = wide[...].astype(BF16)

        pl.run_scoped(with_start, pltpu.VMEM(STACK, F32))


def fetch_own(from_core, rounded, load):
    wait_all(run_copies([(from_core, rounded)], load))


def middle_update(cores, *refs):
    refs = list(refs)
    first = refs.pop(0)
    if not cores:
        refs.pop(0)
    weights = [refs.pop(0) for _ in range(1 if cores else 4)]
    used, outs = refs.pop(0), [refs.pop(0) for _ in range(1 + cores)]
    _, pair, rates, rounded, fresh, e0, e1, hid, e2, sems, load, keep = refs

    @pl.when(lax.rem(lax.axis_index("tm"), 2) == cores)
    def _():
        copies = run_copies(
            [
                (first.at[:, pl.ds(2 * ROWS, 2 * ROWS), :], pair),
                (first.at[:, pl.ds(4 * ROWS, RATE_ROWS), :], rates),
            ],
            keep,
        )
        if cores:
            fetch_own(weights[0], rounded, load)
        else:
            fetch_from_chip(weights[0], weights[1:], rounded, load)
        wait_all(copies)
        kept = pltpu.make_async_copy(rounded, used, keep.at[0])
        kept.start()
        work = (e0, e1, hid, e2)
        errors_of(rounded, pair, rates, 1, work)
        route = functools.partial(piece, outs) if cores else functools.partial(stack_piece, outs[0])
        write_updates(rounded, pair, work, fresh, ((None, route),), sems)
        kept.wait()


def update_middle(cores, first, token, weights):
    operands = [first, *weights] if cores else [first, token, *weights]
    outs = PARTS if cores else [STACK]
    return pl.pallas_call(
        functools.partial(middle_update, cores),
        out_shape=(pltpu.HBM(STACK, BF16), *[pltpu.HBM(shape, BF16) for shape in outs], TOKEN),
        in_specs=[ANY] * len(operands),
        out_specs=(*[HBM] * (1 + len(outs)), HBM),
        scratch_shapes=[
            pltpu.VMEM((HEADS, 2 * ROWS, WIDTH), BF16),
            pltpu.VMEM((HEADS, RATE_ROWS, WIDTH), BF16),
            pltpu.VMEM(STACK, BF16),
            pltpu.VMEM(STACK, BF16),
            *WORK,
            pltpu.SemaphoreType.DMA((6,)),
            pltpu.SemaphoreType.DMA((6,)),
            pltpu.SemaphoreType.DMA((2,)),
        ],
        compiler_params=pltpu.CompilerParams(vmem_limit_bytes=40 * MIB),
        cost_estimate=FREE,
        name="update_tick1_%s" % ("odd" if cores else "even"),
    )(*operands)


def last_update(used, received, first, out, pair, rates, rounded, fresh, e0, e1, hid, e2, sems, load):
    wait_all(
        run_copies(
            [
                (received.at[:, pl.ds(3 * ROWS, 2 * ROWS), :], pair),
                (first.at[:, pl.ds(4 * ROWS, RATE_ROWS), :], rates),
                (used, rounded),
            ],
            load,
        )
    )
    work = (e0, e1, hid, e2)
    errors_of(rounded, pair, rates, 2, work)
    write_updates(rounded, pair, work, fresh, ((None, functools.partial(stack_piece, out)),), sems)


def update_last(used, received, first):
    return pl.pallas_call(
        last_update,
        out_shape=pltpu.HBM(STACK, F32),
        in_specs=[ANY] * 3,
        out_specs=HBM,
        scratch_shapes=[
            pltpu.VMEM((HEADS, 2 * ROWS, WIDTH), BF16),
            pltpu.VMEM((HEADS, RATE_ROWS, WIDTH), BF16),
            pltpu.VMEM(STACK, BF16),
            pltpu.VMEM(STACK, F32),
            *WORK,
            pltpu.SemaphoreType.DMA((6,)),
            pltpu.SemaphoreType.DMA((3,)),
        ],
        compiler_params=pltpu.CompilerParams(vmem_limit_bytes=40 * MIB),
        cost_estimate=FREE,
        name="update_tick2",
    )(used, received, first)


def apply_weights(rounded, query, produced):
    for half in range(2):
        sources = pl.ds(half * 4, 4)
        queries = query[sources, :, :].reshape(HALF, WIDTH)
        gate_part = dot(queries, rounded[0])
        up_part = dot(queries, rounded[1])
        hidden = (gate_part * jax.nn.sigmoid(gate_part) * up_part).astype(BF16)
        produced[sources, :, :] = dot(hidden, rounded[2]).astype(BF16).reshape(4, ROWS, WIDTH)


def first_apply(start, received, out, _, query, wide, rounded, produced, sems):
    copies = run_copies([(start, wide), (received.at[:, slot(0), :], query)], sems)
    copies[0].wait()
    rounded[...] = wide[...].astype(BF16)
    copies[1].wait()
    apply_weights(rounded, query, produced)
    wait_all(run_copies([(produced, out.at[:, slot(0), :])], sems))


def apply_first(start, received):
    return pl.pallas_call(
        first_apply,
        out_shape=(pltpu.HBM((HEADS, 3 * ROWS, WIDTH), BF16), TOKEN),
        in_specs=[ANY] * 2,
        out_specs=(HBM, HBM),
        scratch_shapes=[
            pltpu.VMEM((HEADS, ROWS, WIDTH), BF16),
            pltpu.VMEM(STACK, F32),
            pltpu.VMEM(STACK, BF16),
            pltpu.VMEM((HEADS, ROWS, WIDTH), BF16),
            pltpu.SemaphoreType.DMA((2,)),
        ],
        compiler_params=pltpu.CompilerParams(vmem_limit_bytes=40 * MIB),
        cost_estimate=FREE,
        name="apply_tick0",
    )(start, received)


def middle_apply(used_odd, used_even, received, held, out, _, query, rounded, produced, sems):
    del held
    copies = run_copies([(received.at[:, slot(1), :], query)], sems)
    odd = is_odd()
    pl.when(odd)(lambda: fetch_own(used_odd, rounded, sems.at[pl.ds(1, 1)]))
    pl.when(jnp.logical_not(odd))(lambda: fetch_own(used_even, rounded, sems.at[pl.ds(1, 1)]))
    wait_all(copies)
    apply_weights(rounded, query, produced)
    wait_all(run_copies([(produced, out.at[:, slot(1), :])], sems))


def apply_middle(used_odd, used_even, received, held):
    return pl.pallas_call(
        middle_apply,
        out_shape=(pltpu.HBM((HEADS, 3 * ROWS, WIDTH), BF16), TOKEN),
        in_specs=[ANY] * 4,
        out_specs=(HBM, HBM),
        input_output_aliases={3: 0},
        scratch_shapes=[
            pltpu.VMEM((HEADS, ROWS, WIDTH), BF16),
            pltpu.VMEM(STACK, BF16),
            pltpu.VMEM((HEADS, ROWS, WIDTH), BF16),
            pltpu.SemaphoreType.DMA((2,)),
        ],
        compiler_params=pltpu.CompilerParams(vmem_limit_bytes=40 * MIB),
        cost_estimate=FREE,
        name="apply_tick1",
    )(used_odd, used_even, received, held)


def late_apply(token, start, from_core, direct, straight, relayed, received, held, out, used, query, rounded, produced, sems, load):
    del token, held
    copy = pltpu.make_async_copy(received.at[:, slot(2), :], query, sems.at[0])
    copy.start()
    odd = is_odd()
    pl.when(odd)(lambda: fetch_own(from_core, rounded, load))
    pl.when(jnp.logical_not(odd))(lambda: fetch_from_chip(start, (direct, straight, relayed), rounded, load))
    copy.wait()
    kept = pltpu.make_async_copy(rounded, used, sems.at[1])
    kept.start()
    apply_weights(rounded, query, produced)
    last = pltpu.make_async_copy(produced, out.at[:, slot(2), :], sems.at[0])
    last.start()
    last.wait()
    kept.wait()


def apply_late(token, start, from_core, from_chip, received, held):
    operands = (token, start, from_core, *from_chip, received, held)
    return pl.pallas_call(
        late_apply,
        out_shape=(pltpu.HBM((HEADS, 3 * ROWS, WIDTH), BF16), pltpu.HBM(STACK, BF16)),
        in_specs=[ANY] * len(operands),
        out_specs=(HBM, HBM),
        input_output_aliases={len(operands) - 1: 0},
        scratch_shapes=[
            pltpu.VMEM((HEADS, ROWS, WIDTH), BF16),
            pltpu.VMEM(STACK, BF16),
            pltpu.VMEM((HEADS, ROWS, WIDTH), BF16),
            pltpu.SemaphoreType.DMA((2,)),
            pltpu.SemaphoreType.DMA((6,)),
        ],
        compiler_params=pltpu.CompilerParams(vmem_limit_bytes=40 * MIB),
        cost_estimate=FREE,
        name="apply_tick2",
    )(*operands)


def in_hbm(array):
    return pltpu.with_memory_space_constraint(array, pltpu.HBM)


def exchange(block):
    return lax.all_to_all(block, "head", split_axis=0, concat_axis=0, tiled=True)


def after(*arrays):
    return lax.optimization_barrier(arrays)


def mark_body(first, second, out):
    del first, second, out


def mark(first, second, flops):
    return pl.pallas_call(
        mark_body,
        out_shape=TOKEN,
        in_specs=[HBM, HBM],
        out_specs=HBM,
        cost_estimate=pl.CostEstimate(flops=flops, bytes_accessed=0, transcendentals=0),
        name="mark",
    )(first, second)


def routes_of(places):
    to_core = [(i, i + 1) for i in range(0, places, 2)]
    to_chip = [(i, i + 1) for i in range(1, places - 1, 2)]
    inward, onward = [], []
    for i, j in to_chip:
        for head in range(HEADS):
            if j % PLANE:
                inward.append((i * HEADS + head, j * HEADS + head))
            else:
                relay = i - PLANE + 2 if head < HEADS // 2 else i - PLANE + 4
                inward.append((i * HEADS + head, relay * HEADS + head))
                onward.append((relay * HEADS + head, j * HEADS + head))
    return to_core, to_chip, inward, onward


def on_device(query_rows, key_rows, value_rows, step_rates, start_weights):
    start = in_hbm(start_weights[0, 0])
    to_core, to_chip, inward, onward = routes_of(lax.axis_size("tm"))

    def shift(block, route):
        return lax.ppermute(block, "tm", route)

    def relay(block, route):
        return lax.ppermute(block, ("tm", "head"), route)

    first_sent = send_first(key_rows, value_rows, jnp.swapaxes(step_rates, 1, 2))
    first = in_hbm(exchange(first_sent))
    query_rows, key_rows, value_rows, first_sent = after(query_rows, key_rows, value_rows, first_sent)
    second_sent = send_rest(query_rows, key_rows, value_rows)
    second = in_hbm(exchange(second_sent))

    stacked, part0, part1 = update_start(start, first)
    core1 = shift(stacked, to_core)
    straight1 = relay(part1, inward)
    direct1 = shift(part0, to_chip)
    used_odd, part0, part1, token = update_middle(1, first, None, [core1])
    straight2 = relay(part1, inward)
    direct2 = shift(part0, to_chip)
    straight1, token = after(straight1, token)
    relayed1 = relay(straight1, onward)
    straight2, token = after(straight2, token)
    relayed2 = relay(straight2, onward)
    direct1, token = after(direct1, token)
    relayed1, token = after(relayed1, mark(token, token, 6 * 10**9))
    used_even, stacked, token = update_middle(0, first, token, [start, direct1, straight1, relayed1])
    core2 = shift(stacked, to_core)
    second, token = after(second, token)
    held, _ = apply_first(start, second)
    held, early = apply_middle(used_odd, used_even, second, held)
    direct2, early, token = after(direct2, early, token)
    relayed2, token = after(relayed2, mark(token, early, 3 * 10**9))
    core2, token = after(core2, mark(token, token, 12 * 10**9))
    held, used2 = apply_late(token, start, core2, [direct2, straight2, relayed2], second, held)
    returned = exchange(held)
    final = update_last(used2, second, first)
    result = place_outputs(returned)
    return result, final[None, None]


def solution(mesh):
    return jax.shard_map(
        on_device,
        mesh=mesh,
        in_specs=(
            P(None, ("tm", "head"), None),
            P(None, ("tm", "head"), None),
            P(None, ("tm", "head"), None),
            P(None, ("tm", "head"), None),
            P("tm", "head", None, None, None),
        ),
        out_specs=(P(None, ("tm", "head"), None), P("tm", "head", None, None, None)),
        check_vma=False,
    )
```

```python
import functools

import jax
import jax.numpy as jnp
from jax import lax
from jax.experimental import pallas as pl
from jax.experimental.pallas import tpu as pltpu
from jax.sharding import PartitionSpec as P

HEADS = 8
ROWS = 64
WIDTH = 512
TOKENS = HEADS * ROWS
RATE_ROWS = 16
HALF = TOKENS // 2
F32 = jnp.float32
BF16 = jnp.bfloat16
MIB = 1024 * 1024
FREE = pl.CostEstimate(flops=0, bytes_accessed=0, transcendentals=0)
PLANE = 8
ANY = pl.BlockSpec(memory_space=pl.ANY)
HBM = pl.BlockSpec(memory_space=pltpu.HBM)


def run_copies(pairs, sems):
    copies = [pltpu.make_async_copy(src, dst, sems.at[i]) for i, (src, dst) in enumerate(pairs)]
    for copy in copies:
        copy.start()
    return copies


def wait_all(copies):
    for copy in copies:
        copy.wait()


def head_columns(head):
    return pl.ds(head * WIDTH, WIDTH)


def slot(index):
    return pl.ds(index * ROWS, ROWS)


def pack_arrays(plan, staged, load, store):
    loads = run_copies([(source.at[tick], staged.at[i]) for i, (source, tick, _, _) in enumerate(plan)], load)
    stores = []
    for i, (_, _, target, place) in enumerate(plan):
        loads[i].wait()
        for head in range(HEADS):
            copy = pltpu.make_async_copy(
                staged.at[i, :, head_columns(head)], target.at[head, slot(place), :], store.at[i * HEADS + head]
            )
            copy.start()
            stores.append(copy)
    return stores


def pack_first(keys, values, rates, sent, staged, rate_rows, rate_sent, load, store):
    plan = ((keys, 0, sent, 0), (values, 0, sent, 1), (keys, 1, sent, 2), (values, 1, sent, 3))
    stores = pack_arrays(plan, staged, load, store)
    rate_rows[...] = jnp.zeros_like(rate_rows)
    for tick in range(3):
        turned = rates[tick].astype(F32)
        for head in range(HEADS):
            rate_rows[head, 3 * tick : 3 * tick + 3, 0:ROWS] = turned[3 * head : 3 * head + 3, :]
    rate_sent[...] = rate_rows[...].astype(BF16)
    last = pltpu.make_async_copy(rate_sent, sent.at[:, pl.ds(4 * ROWS, RATE_ROWS), :], store.at[4 * HEADS])
    last.start()
    wait_all(stores)
    last.wait()


def send_first(keys, values, rates):
    return pl.pallas_call(
        pack_first,
        out_shape=pltpu.HBM((HEADS, 4 * ROWS + RATE_ROWS, WIDTH), BF16),
        in_specs=[HBM, HBM, pl.BlockSpec(memory_space=pltpu.VMEM)],
        out_specs=HBM,
        scratch_shapes=[
            pltpu.VMEM((4, ROWS, HEADS * WIDTH), BF16),
            pltpu.VMEM((HEADS, RATE_ROWS, WIDTH), F32),
            pltpu.VMEM((HEADS, RATE_ROWS, WIDTH), BF16),
            pltpu.SemaphoreType.DMA((4,)),
            pltpu.SemaphoreType.DMA((4 * HEADS + 1,)),
        ],
        cost_estimate=FREE,
        name="pack_first",
    )(keys, values, rates)


def pack_rest(queries, keys, values, sent, staged, load, store):
    plan = (
        (queries, 0, sent, 0),
        (queries, 1, sent, 1),
        (queries, 2, sent, 2),
        (keys, 2, sent, 3),
        (values, 2, sent, 4),
    )
    wait_all(pack_arrays(plan, staged, load, store))


def send_rest(queries, keys, values):
    return pl.pallas_call(
        pack_rest,
        out_shape=pltpu.HBM((HEADS, 5 * ROWS, WIDTH), BF16),
        in_specs=[HBM] * 3,
        out_specs=HBM,
        scratch_shapes=[
            pltpu.VMEM((5, ROWS, HEADS * WIDTH), BF16),
            pltpu.SemaphoreType.DMA((5,)),
            pltpu.SemaphoreType.DMA((5 * HEADS,)),
        ],
        cost_estimate=FREE,
        name="pack_rest",
    )(queries, keys, values)


def unpack_arrays(plan, staged, load, store):
    loads = run_copies(
        [
            (source.at[head, slot(place), :], staged.at[i, :, head_columns(head)])
            for i, (source, place, _, _) in enumerate(plan)
            for head in range(HEADS)
        ],
        load,
    )
    stores = []
    for i, (_, _, target, tick) in enumerate(plan):
        wait_all(loads[i * HEADS : (i + 1) * HEADS])
        copy = pltpu.make_async_copy(staged.at[i], target.at[tick], store.at[i])
        copy.start()
        stores.append(copy)
    wait_all(stores)


def unpack_outputs(received, result, staged, load, store):
    unpack_arrays([(received, tick, result, tick) for tick in range(3)], staged, load, store)


def place_outputs(received):
    return pl.pallas_call(
        unpack_outputs,
        out_shape=pltpu.HBM((3, ROWS, HEADS * WIDTH), BF16),
        in_specs=[ANY],
        out_specs=HBM,
        scratch_shapes=[
            pltpu.VMEM((3, ROWS, HEADS * WIDTH), BF16),
            pltpu.SemaphoreType.DMA((3 * HEADS,)),
            pltpu.SemaphoreType.DMA((3,)),
        ],
        compiler_params=pltpu.CompilerParams(vmem_limit_bytes=8 * MIB),
        cost_estimate=FREE,
        name="unpack_outputs",
    )(received)


def dot(left, right, left_dim=1, right_dim=0):
    return lax.dot_general(left, right, (((left_dim,), (right_dim,)), ((), ())), preferred_element_type=F32)


def rate_columns(rates, tick, first_source, sources):
    parts = []
    for source in range(first_source, first_source + sources):
        turned = rates[source, :, 0:128].astype(F32).T
        parts.append(turned[0:ROWS, 3 * tick : 3 * tick + 3])
    return jnp.concatenate(parts, axis=0)


def errors_of(rounded, pair, rates, tick, work):
    gate_error, up_error, hidden, out_error = work
    for half in range(2):
        sources = pl.ds(half * 4, 4)
        rows = pl.ds(half * HALF, HALF)
        keys = pair[sources, 0:ROWS, :].reshape(HALF, WIDTH)
        values = pair[sources, ROWS : 2 * ROWS, :].reshape(HALF, WIDTH)
        rate = rate_columns(rates, tick, half * 4, 4)
        pre_gate = dot(keys, rounded[0])
        pre_up = dot(keys, rounded[1])
        upstream = dot(values, rounded[2], 1, 1)
        sigmoid_value = jax.nn.sigmoid(pre_gate)
        activated = pre_gate * sigmoid_value
        hidden[rows, :] = (activated * pre_up).astype(BF16)
        gate_error[rows, :] = (
            rate[:, 0:1] * upstream * pre_up * sigmoid_value * (1.0 + pre_gate * (1.0 - sigmoid_value))
        ).astype(BF16)
        up_error[rows, :] = (rate[:, 1:2] * upstream * activated).astype(BF16)
        out_error[rows, :] = (rate[:, 2:3] * values.astype(F32)).astype(BF16)


def is_odd():
    return lax.rem(lax.axis_index("tm"), 2) == 1


STACK = (3, WIDTH, WIDTH)
PARTS = ((WIDTH, WIDTH), (2 * WIDTH, WIDTH))
TOKEN = pltpu.HBM((8, 128), F32)


def piece(parts, index, half):
    if index == 0:
        return parts[0].at[pl.ds(half * HALF, HALF), :]
    return parts[1].at[pl.ds((index - 1) * WIDTH + half * HALF, HALF), :]


def stack_piece(stack, index, half):
    return stack.at[index, pl.ds(half * HALF, HALF), :]


def write_updates(added, pair, work, fresh, routes, sems):
    gate_error, up_error, hidden, out_error = work
    started = []
    for index in (1, 2, 0):
        for half in range(2):
            columns = pl.ds(half * HALF, HALF)
            keys = pair[:, 0:ROWS, columns].reshape(TOKENS, HALF)
            left, right = ((keys, gate_error), (keys, up_error), (hidden[:, columns], out_error))[index]
            value = added[index, columns, :].astype(F32) + dot(left, right[...], 0, 0)
            fresh[index, columns, :] = value.astype(fresh.dtype)
            for predicate, target in routes:
                copy = pltpu.make_async_copy(
                    fresh.at[index, columns, :], target(index, half), sems.at[half * 3 + index]
                )
                if predicate is None:
                    copy.start()
                else:
                    pl.when(predicate)(copy.start)
                started.append((predicate, copy))
    for predicate, copy in started:
        if predicate is None:
            copy.wait()
        else:
            pl.when(predicate)(copy.wait)


WORK = [pltpu.VMEM((TOKENS, WIDTH), BF16)] * 4


def start_update(start, received, stacked, part0, part1, pair, rates, wide, rounded, fresh, e0, e1, hid, e2, sems, load):
    copies = run_copies(
        [
            (start, wide),
            (received.at[:, pl.ds(0, 2 * ROWS), :], pair),
            (received.at[:, pl.ds(4 * ROWS, RATE_ROWS), :], rates),
        ],
        load,
    )
    copies[0].wait()
    rounded[...] = wide[...].astype(BF16)
    wait_all(copies[1:])
    work = (e0, e1, hid, e2)
    errors_of(rounded, pair, rates, 0, work)
    odd = is_odd()
    routes = (
        (odd, functools.partial(piece, (part0, part1))),
        (jnp.logical_not(odd), functools.partial(stack_piece, stacked)),
    )
    write_updates(wide, pair, work, fresh, routes, sems)


def update_start(start, received):
    return pl.pallas_call(
        start_update,
        out_shape=tuple(pltpu.HBM(shape, BF16) for shape in (STACK, *PARTS)),
        in_specs=[ANY, ANY],
        out_specs=(HBM,) * 3,
        scratch_shapes=[
            pltpu.VMEM((HEADS, 2 * ROWS, WIDTH), BF16),
            pltpu.VMEM((HEADS, RATE_ROWS, WIDTH), BF16),
            pltpu.VMEM(STACK, F32),
            pltpu.VMEM(STACK, BF16),
            pltpu.VMEM(STACK, BF16),
            *WORK,
            pltpu.SemaphoreType.DMA((6,)),
            pltpu.SemaphoreType.DMA((3,)),
        ],
        compiler_params=pltpu.CompilerParams(vmem_limit_bytes=24 * MIB),
        cost_estimate=FREE,
        name="update_start",
    )(start, received)


def fetch_from_chip(start, from_chip, rounded, load):
    place = lax.axis_index("tm")
    crossed = lax.rem(place, PLANE) == 0
    direct, straight, relayed = from_chip

    def gather(parts):
        order = ((0, 0), (0, 1), (1, 0), (1, 1), (2, 0), (2, 1))
        wait_all(run_copies([(piece(parts, *which), stack_piece(rounded, *which)) for which in order], load))

    pl.when(jnp.logical_not(crossed))(lambda: gather((direct, straight)))
    pl.when(jnp.logical_and(crossed, place > 0))(lambda: gather((direct, relayed)))

    @pl.when(place == 0)
    def _():
        def with_start(wide):
            wait_all(run_copies([(start, wide)], load))
            rounded[...] = wide[...].astype(BF16)

        pl.run_scoped(with_start, pltpu.VMEM(STACK, F32))


def fetch_own(from_core, rounded, load):
    wait_all(run_copies([(from_core, rounded)], load))


def middle_update(cores, *refs):
    refs = list(refs)
    first = refs.pop(0)
    if not cores:
        refs.pop(0)
    weights = [refs.pop(0) for _ in range(1 if cores else 4)]
    used, outs = refs.pop(0), [refs.pop(0) for _ in range(1 + cores)]
    _, pair, rates, rounded, fresh, e0, e1, hid, e2, sems, load, keep = refs

    @pl.when(lax.rem(lax.axis_index("tm"), 2) == cores)
    def _():
        copies = run_copies(
            [
                (first.at[:, pl.ds(2 * ROWS, 2 * ROWS), :], pair),
                (first.at[:, pl.ds(4 * ROWS, RATE_ROWS), :], rates),
            ],
            keep,
        )
        if cores:
            fetch_own(weights[0], rounded, load)
        else:
            fetch_from_chip(weights[0], weights[1:], rounded, load)
        wait_all(copies)
        kept = pltpu.make_async_copy(rounded, used, keep.at[0])
        kept.start()
        work = (e0, e1, hid, e2)
        errors_of(rounded, pair, rates, 1, work)
        route = functools.partial(piece, outs) if cores else functools.partial(stack_piece, outs[0])
        write_updates(rounded, pair, work, fresh, ((None, route),), sems)
        kept.wait()


def update_middle(cores, first, token, weights):
    operands = [first, *weights] if cores else [first, token, *weights]
    outs = PARTS if cores else [STACK]
    return pl.pallas_call(
        functools.partial(middle_update, cores),
        out_shape=(pltpu.HBM(STACK, BF16), *[pltpu.HBM(shape, BF16) for shape in outs], TOKEN),
        in_specs=[ANY] * len(operands),
        out_specs=(*[HBM] * (1 + len(outs)), HBM),
        scratch_shapes=[
            pltpu.VMEM((HEADS, 2 * ROWS, WIDTH), BF16),
            pltpu.VMEM((HEADS, RATE_ROWS, WIDTH), BF16),
            pltpu.VMEM(STACK, BF16),
            pltpu.VMEM(STACK, BF16),
            *WORK,
            pltpu.SemaphoreType.DMA((6,)),
            pltpu.SemaphoreType.DMA((6,)),
            pltpu.SemaphoreType.DMA((2,)),
        ],
        compiler_params=pltpu.CompilerParams(vmem_limit_bytes=24 * MIB),
        cost_estimate=FREE,
        name="update_tick1_%s" % ("odd" if cores else "even"),
    )(*operands)


def last_update(used, received, first, out, pair, rates, rounded, fresh, e0, e1, hid, e2, sems, load):
    wait_all(
        run_copies(
            [
                (received.at[:, pl.ds(3 * ROWS, 2 * ROWS), :], pair),
                (first.at[:, pl.ds(4 * ROWS, RATE_ROWS), :], rates),
                (used, rounded),
            ],
            load,
        )
    )
    work = (e0, e1, hid, e2)
    errors_of(rounded, pair, rates, 2, work)
    write_updates(rounded, pair, work, fresh, ((None, functools.partial(stack_piece, out)),), sems)


def update_last(used, received, first):
    return pl.pallas_call(
        last_update,
        out_shape=pltpu.HBM(STACK, F32),
        in_specs=[ANY] * 3,
        out_specs=HBM,
        scratch_shapes=[
            pltpu.VMEM((HEADS, 2 * ROWS, WIDTH), BF16),
            pltpu.VMEM((HEADS, RATE_ROWS, WIDTH), BF16),
            pltpu.VMEM(STACK, BF16),
            pltpu.VMEM(STACK, F32),
            *WORK,
            pltpu.SemaphoreType.DMA((6,)),
            pltpu.SemaphoreType.DMA((3,)),
        ],
        compiler_params=pltpu.CompilerParams(vmem_limit_bytes=24 * MIB),
        cost_estimate=FREE,
        name="update_tick2",
    )(used, received, first)


def apply_weights(rounded, query, produced):
    for half in range(2):
        sources = pl.ds(half * 4, 4)
        queries = query[sources, :, :].reshape(HALF, WIDTH)
        gate_part = dot(queries, rounded[0])
        up_part = dot(queries, rounded[1])
        hidden = (gate_part * jax.nn.sigmoid(gate_part) * up_part).astype(BF16)
        produced[sources, :, :] = dot(hidden, rounded[2]).astype(BF16).reshape(4, ROWS, WIDTH)


def early_apply(start, used_odd, used_even, received, out, _, query, wide, rounded, produced, loads):
    queries = run_copies([(received.at[:, slot(tick), :], query.at[tick]) for tick in range(2)], loads)
    odd = is_odd()
    even = jnp.logical_not(odd)
    later = [pltpu.make_async_copy(source, rounded.at[1], loads.at[2]) for source in (used_even, used_odd)]
    pl.when(even)(later[0].start)
    pl.when(odd)(later[1].start)
    first = pltpu.make_async_copy(start, wide, loads.at[3])
    first.start()
    stores = []

    def finish(tick):
        queries[tick].wait()
        apply_weights(rounded.at[tick], query.at[tick], produced.at[tick])
        store = pltpu.make_async_copy(produced.at[tick], out.at[:, slot(tick), :], loads.at[tick])
        store.start()
        stores.append(store)

    pl.when(even)(later[0].wait)
    pl.when(odd)(later[1].wait)
    finish(1)
    first.wait()
    rounded[0] = wide[...].astype(BF16)
    finish(0)
    wait_all(stores)


def apply_early(*operands):
    return pl.pallas_call(
        early_apply,
        out_shape=(pltpu.HBM((HEADS, 3 * ROWS, WIDTH), BF16), TOKEN),
        in_specs=[ANY] * len(operands),
        out_specs=(HBM, HBM),
        scratch_shapes=[
            pltpu.VMEM((2, HEADS, ROWS, WIDTH), BF16),
            pltpu.VMEM(STACK, F32),
            pltpu.VMEM((2, *STACK), BF16),
            pltpu.VMEM((2, HEADS, ROWS, WIDTH), BF16),
            pltpu.SemaphoreType.DMA((4,)),
        ],
        compiler_params=pltpu.CompilerParams(vmem_limit_bytes=24 * MIB),
        cost_estimate=FREE,
        name="apply_ticks01",
    )(*operands)


def late_apply(token, start, from_core, direct, straight, relayed, received, held, out, used, query, rounded, produced, sems, load):
    del token, held
    copy = pltpu.make_async_copy(received.at[:, slot(2), :], query, sems.at[0])
    copy.start()
    odd = is_odd()
    pl.when(odd)(lambda: fetch_own(from_core, rounded, load))
    pl.when(jnp.logical_not(odd))(lambda: fetch_from_chip(start, (direct, straight, relayed), rounded, load))
    copy.wait()
    kept = pltpu.make_async_copy(rounded, used, sems.at[1])
    kept.start()
    apply_weights(rounded, query, produced)
    last = pltpu.make_async_copy(produced, out.at[:, slot(2), :], sems.at[0])
    last.start()
    last.wait()
    kept.wait()


def apply_late(token, start, from_core, from_chip, received, held):
    operands = (token, start, from_core, *from_chip, received, held)
    return pl.pallas_call(
        late_apply,
        out_shape=(pltpu.HBM((HEADS, 3 * ROWS, WIDTH), BF16), pltpu.HBM(STACK, BF16)),
        in_specs=[ANY] * len(operands),
        out_specs=(HBM, HBM),
        input_output_aliases={len(operands) - 1: 0},
        scratch_shapes=[
            pltpu.VMEM((HEADS, ROWS, WIDTH), BF16),
            pltpu.VMEM(STACK, BF16),
            pltpu.VMEM((HEADS, ROWS, WIDTH), BF16),
            pltpu.SemaphoreType.DMA((2,)),
            pltpu.SemaphoreType.DMA((6,)),
        ],
        compiler_params=pltpu.CompilerParams(vmem_limit_bytes=24 * MIB),
        cost_estimate=FREE,
        name="apply_tick2",
    )(*operands)


def in_hbm(array):
    return pltpu.with_memory_space_constraint(array, pltpu.HBM)


def exchange(block):
    return lax.all_to_all(block, "head", split_axis=0, concat_axis=0, tiled=True)


def after(*arrays):
    return lax.optimization_barrier(arrays)


def mark_body(first, second, out):
    del first, second, out


def mark(first, second, flops):
    return pl.pallas_call(
        mark_body,
        out_shape=TOKEN,
        in_specs=[HBM, HBM],
        out_specs=HBM,
        cost_estimate=pl.CostEstimate(flops=flops, bytes_accessed=0, transcendentals=0),
        name="mark",
    )(first, second)


def routes_of(places):
    to_core = [(i, i + 1) for i in range(0, places, 2)]
    to_chip = [(i, i + 1) for i in range(1, places - 1, 2)]
    inward, onward = [], []
    for i, j in to_chip:
        for head in range(HEADS):
            if j % PLANE:
                inward.append((i * HEADS + head, j * HEADS + head))
            else:
                relay = i - PLANE + 2 if head < HEADS // 2 else i - PLANE + 4
                inward.append((i * HEADS + head, relay * HEADS + head))
                onward.append((relay * HEADS + head, j * HEADS + head))
    return to_core, to_chip, inward, onward


def on_device(query_rows, key_rows, value_rows, step_rates, start_weights):
    start = in_hbm(start_weights[0, 0])
    to_core, to_chip, inward, onward = routes_of(lax.axis_size("tm"))

    def shift(block, route):
        return lax.ppermute(block, "tm", route)

    def relay(block, route):
        return lax.ppermute(block, ("tm", "head"), route)

    first_sent = send_first(key_rows, value_rows, jnp.swapaxes(step_rates, 1, 2))
    first = exchange(first_sent)
    query_rows, key_rows, value_rows, first_sent = after(query_rows, key_rows, value_rows, first_sent)
    second_sent = send_rest(query_rows, key_rows, value_rows)
    second = in_hbm(exchange(second_sent))

    stacked, part0, part1 = update_start(start, first)
    core1 = shift(stacked, to_core)
    straight1 = relay(part1, inward)
    direct1 = shift(part0, to_chip)
    used_odd, part0, part1, token = update_middle(1, first, None, [core1])
    straight2 = relay(part1, inward)
    direct2 = shift(part0, to_chip)
    straight1, token = after(straight1, token)
    relayed1 = relay(straight1, onward)
    straight2, token = after(straight2, token)
    relayed2 = relay(straight2, onward)
    direct1, token = after(direct1, token)
    relayed1, token = after(relayed1, mark(token, token, 6 * 10**9))
    used_even, stacked, token = update_middle(0, first, in_hbm(token), [start, direct1, straight1, relayed1])
    core2 = shift(stacked, to_core)
    second, token = after(second, token)
    held, early = apply_early(start, in_hbm(used_odd), in_hbm(used_even), second)
    direct2, early, token = after(direct2, early, token)
    relayed2, token = after(relayed2, mark(token, early, 3 * 10**9))
    core2, token = after(core2, mark(token, token, 12 * 10**9))
    held, used2 = apply_late(in_hbm(token), start, core2, [direct2, straight2, relayed2], second, held)
    returned = exchange(held)
    final = update_last(in_hbm(used2), second, first)
    result = place_outputs(returned)
    return result, final[None, None]


def solution(mesh):
    return jax.shard_map(
        on_device,
        mesh=mesh,
        in_specs=(
            P(None, ("tm", "head"), None),
            P(None, ("tm", "head"), None),
            P(None, ("tm", "head"), None),
            P(None, ("tm", "head"), None),
            P("tm", "head", None, None, None),
        ),
        out_specs=(P(None, ("tm", "head"), None), P("tm", "head", None, None, None)),
        check_vma=False,
    )
```
